512 devices in a mesh: dp: 16 (over z, core), latent: 32 (over x, y).
Axes of the slice: x: 4, y: 8, z: 8, core: 2. Of those that a mesh axis runs over, the one named last changes fastest.
Arguments:
- activations: bfloat16 [16384, 8192], P('latent', 'dp'), may hold values from -6 to 6
- weight: bfloat16 [8192, 8192], P('dp', 'latent'), may hold values from -0.0625 to 0.0625
- enc_bias: float32 [8192], replicated, may hold values from -3 to 3
- dec_bias: float32 [8192], P('dp'), may hold values from -3 to 3
- block_ids: int32 [32, 8], P('latent'), may hold values from 0 to 63, as said below
- counts: int32 [32], P('latent'), may hold values from 1 to 8, as said below
Outputs:
- weight_grad: float32 [8192, 8192], P('dp', 'latent')
- row_error: float32 [16384], P(('latent', 'dp'))
The draws below stay inside these ranges and needn't reach their ends.
Inputs may be any that keep to these rules, and one draw needn't show every extreme that they name: `block_ids`: each row block's list names 8 latent blocks of 8 different owners (block k belongs to owner k // 2); only its first counts entries are active, and some blocks are listed far more often than others. `counts`: some row block has all 8 entries active.
All inputs are finite; a program needn't handle non-finite values.
Results may differ from the reference program's by a relative error of at most 0.0028.
Values may be sent and summed in bfloat16 or wider, within the bound.
No kernel may reach another device: no remote copies, remote signals or barrier semaphores. Data moves between devices by JAX's collectives and lax.ppermute only.
A program may use at most 64 MiB of HBM per device.

```python
import math
import jax
import jax.numpy as jnp
from jax import lax

D = 8192
BLK = 128
BLK_DEV = 2
K_MAX = 8
RB = 512
ROW_BLOCK_COUNT = 32
NBLK = 64
LATENTS = 8192
ROWS = 16384
N_DP = 16


def lists_common(key):
    base = jax.random.fold_in(key, 7)
    keys = jax.random.split(base, 6)
    usage_frequency = jax.random.randint(keys[0], (ROW_BLOCK_COUNT,), 0, 4)
    usage_frequency = usage_frequency * usage_frequency
    random_jitter = jax.random.randint(keys[1], (ROW_BLOCK_COUNT, ROW_BLOCK_COUNT), 0, 65536)
    picked = jax.random.randint(keys[4], (), 0, ROW_BLOCK_COUNT)
    row_index = jnp.arange(ROW_BLOCK_COUNT, dtype=jnp.int32)
    column_position_index = jnp.arange(ROW_BLOCK_COUNT, dtype=jnp.int32)
    ending_row = (row_index == picked).astype(jnp.int32)[:, None] * (column_position_index == ROW_BLOCK_COUNT - 1).astype(jnp.int32)[None, :]
    starting_row = (row_index == (picked + 1) % ROW_BLOCK_COUNT).astype(jnp.int32)[:, None] * (column_position_index == 0).astype(jnp.int32)[None, :]
    extra_reward = (ending_row + starting_row) * 262144
    ranking_value = (random_jitter + usage_frequency[None, :] * 16384 + extra_reward) * ROW_BLOCK_COUNT + column_position_index[None, :]
    unused, chosen = lax.top_k(ranking_value.astype(jnp.int32), K_MAX)
    inner_all = jax.random.randint(keys[5], (ROW_BLOCK_COUNT, ROW_BLOCK_COUNT), 0, BLK_DEV)
    inner_all = jnp.where(ending_row > 0, BLK_DEV - 1, inner_all)
    inner_all = jnp.where(starting_row > 0, 0, inner_all)
    inner = jnp.take_along_axis(inner_all, chosen.astype(jnp.int32), axis=1)
    chosen_ids = chosen.astype(jnp.int32) * BLK_DEV + inner
    first_draw = jax.random.randint(keys[2], (ROW_BLOCK_COUNT,), 0, K_MAX)
    second_draw = jax.random.randint(keys[3], (ROW_BLOCK_COUNT,), 0, K_MAX)
    active = 1 + jnp.minimum(first_draw, second_draw)
    active = jnp.where(row_index == picked, K_MAX, active)
    return (chosen_ids.astype(jnp.int32), active.astype(jnp.int32))


def draw_block_ids(key, part):
    return lists_common(key)[0]


def draw_counts(key, part):
    return lists_common(key)[1]


def steps_of(own_key, extent, pieces, least, largest):
    level = 1.0
    for dim, blocks in pieces:
        steps = jax.random.uniform(jax.random.fold_in(jax.random.fold_in(own_key, 6), dim), (blocks,), jnp.float32, least / len(pieces), largest / len(pieces))
        level = level * jnp.repeat(jnp.exp(steps), extent[dim] // blocks).reshape((-1,) + (1,) * (len(extent) - 1 - dim))
    return level


def centred(stream_key, dims, spread, reach, cuts=(), kind=jnp.bfloat16):
    gain = steps_of(stream_key, dims, cuts, -0.22, 0.18) if cuts else 1.0
    drawn = jax.random.normal(stream_key, dims, jnp.float32) * spread * gain
    return jnp.minimum(jnp.maximum(drawn, -reach), reach).astype(kind)


def setup_inputs(seed: int = 0) -> dict:
    streams_of = jax.random.split(jax.random.key(seed), 7)
    activations = centred(streams_of[0], (ROWS, D), 1.0, 6.0, ((0, 32), (1, 16)))
    weight = centred(streams_of[1], (D, LATENTS), D ** -0.5, 0.0625, ((0, 16), (1, 32)))
    enc_bias = centred(streams_of[2], (LATENTS,), 0.5, 3.0, (), jnp.float32)
    dec_bias = centred(streams_of[3], (D,), 0.5, 3.0, ((0, 16),), jnp.float32)
    block_ids = draw_block_ids(jax.random.fold_in(streams_of[6], 71), 0)
    counts = draw_counts(jax.random.fold_in(streams_of[6], 71), 0)
    return {"activations": activations, "weight": weight, "enc_bias": enc_bias, "dec_bias": dec_bias, "block_ids": block_ids, "counts": counts}


def reference(activations, weight, enc_bias, dec_bias, block_ids, counts):
    groups = N_DP
    width = D // groups
    scale_grad = 2.0 / math.sqrt(RB * ROW_BLOCK_COUNT)
    tiles_all = weight.reshape(D, NBLK, BLK)
    bias_all = enc_bias.reshape(NBLK, BLK)

    def one_block(carry, item):
        rows_x, ids, count = item
        live = (jnp.arange(K_MAX) < count).astype(jnp.float32)[:, None, None]
        centered = (rows_x.astype(jnp.float32) - dec_bias).astype(jnp.bfloat16)
        tiles = jnp.take(tiles_all, ids, axis=1).astype(jnp.float32)
        tiles_split = tiles.reshape(groups, width, K_MAX, BLK)
        cen_split = centered.astype(jnp.float32).reshape(RB, groups, width)
        part_pre = jnp.einsum('rqd,qdsk->qsrk', cen_split, tiles_split)
        pre = lax.optimization_barrier(jnp.sum(part_pre, axis=0)) + jnp.take(bias_all, ids, axis=0)[:, None, :]
        act = (jnp.maximum(pre, 0.0) * live).astype(jnp.bfloat16)
        recon = jnp.einsum('srk,dsk->rd', act.astype(jnp.float32), tiles) + dec_bias
        err = recon - rows_x.astype(jnp.float32)
        grad_out = (err * scale_grad).astype(jnp.bfloat16)
        part_loss = lax.optimization_barrier(jnp.sum((err * err).reshape(RB, groups, width), axis=2)) / D
        row_err = lax.optimization_barrier(jnp.sum(part_loss, axis=1))
        out_split = grad_out.astype(jnp.float32).reshape(RB, groups, width)
        part_grad = jnp.einsum('rqd,qdsk->qsrk', out_split, tiles_split)
        grad_act = lax.optimization_barrier(jnp.sum(part_grad, axis=0))
        grad_pre = (jnp.where(pre > 0, grad_act, 0.0) * live).astype(jnp.bfloat16)
        first = jnp.einsum('rd,srk->dsk', centered.astype(jnp.float32), grad_pre.astype(jnp.float32))
        second = jnp.einsum('rd,srk->dsk', grad_out.astype(jnp.float32), act.astype(jnp.float32))
        contribution = (first + second).astype(jnp.bfloat16).astype(jnp.float32) * live[:, 0, 0][None, :, None]
        carry = carry.at[:, ids, :].add(contribution)
        return (carry, row_err)
    init = jnp.zeros((D, NBLK, BLK), jnp.float32)
    items = (activations.reshape(ROW_BLOCK_COUNT, RB, D), block_ids.astype(jnp.int32), counts.astype(jnp.int32))
    total, errors = lax.scan(one_block, init, items)
    return (total.reshape(D, NBLK * BLK), errors.reshape(ROW_BLOCK_COUNT * RB))
```

```python
import functools
import math

import jax
import jax.numpy as jnp
from jax import lax
from jax.experimental import pallas as pl
from jax.experimental.pallas import tpu as pltpu
from jax.sharding import PartitionSpec as P

BLK = 128
BF16 = jnp.bfloat16
F32 = jnp.float32
VMEM_LIMIT = 40 * 1024 * 1024
SMEM_SPEC = pl.BlockSpec(memory_space=pltpu.SMEM)
VMEM_SPEC = pl.BlockSpec(memory_space=pltpu.VMEM)
ANY_SPEC = pl.BlockSpec(memory_space=pl.ANY)


def contract(a, b, dim_a, dim_b):
    return lax.dot_general(a, b, (((dim_a,), (dim_b,)), ((), ())), preferred_element_type=F32)


def call(kernel, out_shape, in_specs, out_specs, flops=0, bytes_accessed=0, scratch=(), **more):
    return pl.pallas_call(
        kernel,
        out_shape=out_shape,
        in_specs=in_specs,
        out_specs=out_specs,
        scratch_shapes=list(scratch),
        compiler_params=pltpu.CompilerParams(vmem_limit_bytes=VMEM_LIMIT),
        cost_estimate=pl.CostEstimate(
            flops=flops, bytes_accessed=bytes_accessed, transcendentals=0
        ),
        **more,
    )


def encode_kernel(slots, ids, give_x, keep_x, head, tail, give, keep, tiles, sems):
    cut = head.shape[1]
    copies = []
    for s in range(slots):
        owner = ids[s] // 2
        lane = pl.multiple_of((ids[s] % 2) * BLK, BLK)
        columns = pl.ds(s * BLK, BLK)
        one = pltpu.make_async_copy(
            head.at[owner], tiles.at[pl.ds(0, cut), columns], sems.at[2 * s]
        )
        two = pltpu.make_async_copy(
            tail.at[owner, :, pl.ds(lane, BLK)],
            tiles.at[pl.ds(cut, tail.shape[1]), columns],
            sems.at[2 * s + 1],
        )
        one.start()
        two.start()
        copies.append((one, two))
    for s in range(0, slots, 2):
        for pair in copies[s : s + 2]:
            for copy in pair:
                copy.wait()
        columns = slice(s * BLK, (s + 2) * BLK)
        part = tiles[:, columns]
        give[:, columns] = contract(give_x[...], part, 1, 0)
        keep[:, columns] = contract(keep_x[...], part, 1, 0)


def activate_kernel(parts, bias, live, pre, spread):
    total = jnp.sum(parts[...], axis=0) + bias[...]
    pre[...] = total
    act = (jnp.maximum(total, 0.0) * live[...]).astype(BF16)
    spread[...] = jnp.broadcast_to(act[None], spread.shape)


def error_kernel(scale, loss_scale, act_g, act_k, tiles, x_g, x_k, bias, give, keep, out_g, out_k):
    latents = tiles.shape[1]
    for act, x, part, out in ((act_g, x_g, give, out_g), (act_k, x_k, keep, out_k)):
        err = contract(act[...], tiles[...], 1, 1) + bias[...] - x[...].astype(F32)
        loss = jnp.sum(err * err, axis=1, keepdims=True) * loss_scale
        grad = (err * scale).astype(BF16)
        out[...] = grad
        part[:, :latents] = contract(grad, tiles[...], 1, 0)
        part[:, latents:] = jnp.broadcast_to(loss, (loss.shape[0], BLK))


def second_kernel(out_g, out_k, act_g, act_k, second):
    latents = act_g.shape[1]
    for start in range(0, latents, 2 * BLK):
        columns = slice(start, start + 2 * BLK)
        second[:, columns] = contract(out_k[...], act_k[:, columns], 0, 0) + contract(
            out_g[...], act_g[:, columns], 0, 0
        )


def gate_kernel(parts, pre, live, spread, loss):
    latents = pre.shape[1]
    total = jnp.sum(parts[...], axis=0)
    grad = (jnp.where(pre[...] > 0, total[:, :latents], 0.0) * live[...]).astype(BF16)
    spread[...] = jnp.broadcast_to(grad[None], spread.shape)
    loss[...] = total[:, latents:]


def contribution_kernel(slots, ids, c_t, gp_g, gp_k, second, send, stage, sems):
    half = gp_g.shape[0]
    copies = []
    for s in range(0, slots, 2):
        columns = slice(s * BLK, (s + 2) * BLK)
        total = (
            contract(c_t[:, :half], gp_g[:, columns], 1, 0)
            + contract(c_t[:, half:], gp_k[:, columns], 1, 0)
            + second[:, columns]
        ).astype(BF16)
        for i in range(2):
            stage[s + i] = total[:, i * BLK : (i + 1) * BLK]
            copy = pltpu.make_async_copy(
                stage.at[s + i], send.at[ids[s + i] // 2], sems.at[s + i]
            )
            copy.start()
            copies.append(copy)
    for copy in copies:
        copy.wait()


def collect_kernel(owners, flags, parts, out):
    out[...] = jnp.zeros_like(out)

    def step(j, carry):
        flag = flags[j]
        for b in range(2):

            @pl.when(flag == b)
            def _():
                out[:, b * BLK : (b + 1) * BLK] += parts[j].astype(F32)

        return carry

    lax.fori_loop(0, owners, step, 0)


def on_device(activations, weight, enc_bias, dec_bias, block_ids, counts):
    rows, width = activations.shape
    owners = lax.axis_size("latent")
    groups = lax.axis_size("dp")
    share = rows // groups
    chips = groups // 2
    half = rows // 2
    slots = block_ids.shape[1]
    latents = slots * BLK
    myself = lax.axis_index("latent")
    core = lax.axis_index("dp") % 2
    same_core = [[2 * z + c for z in range(chips)] for c in range(2)]
    swap = [(q, q ^ 1) for q in range(groups)]
    cut = width * 5 // 8

    def across_chips(array):
        return lax.all_to_all(array, "dp", 0, 0, tiled=True, axis_index_groups=same_core)

    def shape(dims, dtype):
        return jax.ShapeDtypeStruct(dims, dtype)

    tail = lax.all_gather(weight[cut:], "latent", axis=0)

    ids = block_ids[0]
    note = jnp.concatenate([ids, counts])
    note = jnp.pad(note, (0, BLK - slots - 1))
    notes = lax.all_to_all(
        jnp.broadcast_to(note, (owners, 8, BLK)), "latent", 0, 0, tiled=True
    )[:, 0, :]
    all_ids = notes[:, :slots]
    all_counts = notes[:, slots]
    all_live = jnp.arange(slots)[None, :] < all_counts[:, None]
    mine = all_ids // 2 == myself
    upper = jnp.any(mine & (all_ids % 2 == 1), axis=1)
    flags = jnp.sum(jnp.where(mine & all_live, all_ids % 2 + 1, 0), axis=1) - 1

    head = jnp.where(upper[:, None, None], weight[None, :cut, BLK:], weight[None, :cut, :BLK])
    head = lax.all_to_all(head, "latent", 0, 0, tiled=True)

    live = (jnp.arange(slots) < counts[0]).astype(F32)
    live_row = jnp.repeat(live, BLK)[None, :]
    bias_row = jnp.take(enc_bias.reshape(-1, BLK), ids, axis=0).reshape(1, latents)
    by_chunk = activations.reshape(chips, 2, share, width)
    x_k = lax.dynamic_index_in_dim(by_chunk, core, 1, keepdims=False).reshape(half, width)
    x_g = lax.dynamic_index_in_dim(by_chunk, 1 - core, 1, keepdims=False).reshape(half, width)
    c_k = (x_k.astype(F32) - dec_bias).astype(BF16)
    c_g = (x_g.astype(F32) - dec_bias).astype(BF16)
    c_t = jnp.concatenate([c_g, c_k], axis=0).T

    matmul = 2 * half * width * latents
    give, keep, tiles = call(
        functools.partial(encode_kernel, slots),
        (shape((half, latents), F32), shape((half, latents), F32), shape((width, latents), BF16)),
        [SMEM_SPEC, VMEM_SPEC, VMEM_SPEC, ANY_SPEC, ANY_SPEC],
        (VMEM_SPEC, VMEM_SPEC, VMEM_SPEC),
        flops=2 * matmul,
        bytes_accessed=4 * half * latents * 4,
        scratch=[pltpu.SemaphoreType.DMA((2 * slots,))],
    )(ids, c_g, c_k, head, tail)

    keep = keep + lax.ppermute(give, "dp", swap)
    parts = across_chips(keep.reshape(chips, share, latents))
    pre, spread = call(
        activate_kernel,
        (shape((share, latents), F32), shape((chips, share, latents), BF16)),
        [VMEM_SPEC] * 3,
        (VMEM_SPEC, VMEM_SPEC),
        bytes_accessed=half * latents * 6,
    )(parts, bias_row, live_row)
    act_k = across_chips(spread).reshape(half, latents)
    act_g = lax.ppermute(act_k, "dp", swap)

    scale = 2.0 / math.sqrt(rows * owners)
    give, keep, out_g, out_k = call(
        functools.partial(error_kernel, scale, 1.0 / (width * groups)),
        (
            shape((half, latents + BLK), F32),
            shape((half, latents + BLK), F32),
            shape((half, width), BF16),
            shape((half, width), BF16),
        ),
        [VMEM_SPEC] * 6,
        (VMEM_SPEC,) * 4,
        flops=4 * matmul,
        bytes_accessed=half * latents * 14,
    )(act_g, act_k, tiles, x_g, x_k, dec_bias[None, :])
    keep = keep + lax.ppermute(give, "dp", swap)
    parts = across_chips(keep.reshape(chips, share, latents + BLK))
    second = call(
        second_kernel,
        shape((width, latents), F32),
        [VMEM_SPEC] * 4,
        VMEM_SPEC,
        flops=2 * matmul,
        bytes_accessed=half * latents * 16,
    )(out_g, out_k, act_g, act_k)
    spread, loss = call(
        gate_kernel,
        (shape((chips, share, latents), BF16), shape((share, BLK), F32)),
        [VMEM_SPEC] * 3,
        (VMEM_SPEC, VMEM_SPEC),
        bytes_accessed=half * latents * 6,
    )(parts, pre, live_row)
    row_error = loss[:, 0]
    gp_k = across_chips(spread).reshape(half, latents)
    gp_g = lax.ppermute(gp_k, "dp", swap)

    send = call(
        functools.partial(contribution_kernel, slots),
        shape((owners, width, BLK), BF16),
        [SMEM_SPEC] + [VMEM_SPEC] * 4,
        ANY_SPEC,
        flops=2 * matmul,
        bytes_accessed=half * latents * 16,
        scratch=[pltpu.VMEM((slots, width, BLK), BF16), pltpu.SemaphoreType.DMA((slots,))],
    )(ids, c_t, gp_g, gp_k, second)
    received = lax.all_to_all(send, "latent", 0, 0, tiled=True)

    chunk = min(width, 128)
    weight_grad = pl.pallas_call(
        functools.partial(collect_kernel, owners),
        grid=(width // chunk,),
        in_specs=[SMEM_SPEC, pl.BlockSpec((owners, chunk, BLK), lambda i: (0, i, 0))],
        out_specs=pl.BlockSpec((chunk, 2 * BLK), lambda i: (i, 0)),
        out_shape=shape((width, 2 * BLK), F32),
        compiler_params=pltpu.CompilerParams(vmem_limit_bytes=VMEM_LIMIT),
        cost_estimate=pl.CostEstimate(
            flops=owners * width * BLK, bytes_accessed=owners * width * BLK * 2, transcendentals=0
        ),
    )(flags, received)
    return (weight_grad, row_error)


def solution(mesh):
    placed = (P("latent", "dp"), P("dp", "latent"), P(), P("dp"), P("latent", None), P("latent"))
    return jax.shard_map(
        on_device,
        mesh=mesh,
        in_specs=placed,
        out_specs=(P("dp", "latent"), P(("latent", "dp"))),
        check_vma=False,
    )
```

```python
import functools
import math

import jax
import jax.numpy as jnp
from jax import lax
from jax.experimental import pallas as pl
from jax.experimental.pallas import tpu as pltpu
from jax.sharding import PartitionSpec as P

BLK = 128
BF16 = jnp.bfloat16
F32 = jnp.float32
VMEM_LIMIT = 40 * 1024 * 1024
SMEM_SPEC = pl.BlockSpec(memory_space=pltpu.SMEM)
VMEM_SPEC = pl.BlockSpec(memory_space=pltpu.VMEM)
ANY_SPEC = pl.BlockSpec(memory_space=pl.ANY)
HBM_SPEC = pl.BlockSpec(memory_space=pltpu.HBM)


def contract(a, b, dim_a, dim_b):
    return lax.dot_general(a, b, (((dim_a,), (dim_b,)), ((), ())), preferred_element_type=F32)


def call(kernel, out_shape, in_specs, out_specs, flops=0, bytes_accessed=0, scratch=(), **more):
    return pl.pallas_call(
        kernel,
        out_shape=out_shape,
        in_specs=in_specs,
        out_specs=out_specs,
        scratch_shapes=list(scratch),
        compiler_params=pltpu.CompilerParams(vmem_limit_bytes=VMEM_LIMIT),
        cost_estimate=pl.CostEstimate(
            flops=flops, bytes_accessed=bytes_accessed, transcendentals=0
        ),
        **more,
    )


def prepare_kernel(which, x, bias, x_g, x_k, c_g, c_k, c_t):
    half = x_g.shape[0]
    core = which[0]
    for i, (part, out) in enumerate(((x_g, c_g), (x_k, c_k))):
        rows = x[:, (1 - core) if i == 0 else core].reshape(part.shape)
        part[...] = rows
        centered = rows.astype(F32) - bias[...]
        out[...] = centered.astype(BF16)
        c_t[:, i * half : (i + 1) * half] = centered.T.astype(BF16)


def encode_kernel(slots, ids, give_x, keep_x, blocks, give, keep, tiles, sems):
    copies = []
    for s in range(slots):
        copy = pltpu.make_async_copy(
            blocks.at[ids[s] // 2], tiles.at[:, pl.ds(s * BLK, BLK)], sems.at[s]
        )
        copy.start()
        copies.append(copy)
    for s in range(0, slots, 2):
        for copy in copies[s : s + 2]:
            copy.wait()
        columns = slice(s * BLK, (s + 2) * BLK)
        part = tiles[:, columns]
        give[:, columns] = contract(give_x[...], part, 1, 0)
        keep[:, columns] = contract(keep_x[...], part, 1, 0)


def activate_kernel(parts, bias, live, pre, spread):
    total = jnp.sum(parts[...], axis=0) + bias[...]
    pre[...] = total
    act = (jnp.maximum(total, 0.0) * live[...]).astype(BF16)
    spread[...] = jnp.broadcast_to(act[None], spread.shape)


def error_kernel(scale, loss_scale, act_g, act_k, tiles, x_g, x_k, bias, give, keep, out_g, out_k):
    latents = tiles.shape[1]
    for act, x, part, out in ((act_g, x_g, give, out_g), (act_k, x_k, keep, out_k)):
        err = contract(act[...], tiles[...], 1, 1) + bias[...] - x[...].astype(F32)
        loss = jnp.sum(err * err, axis=1, keepdims=True) * loss_scale
        grad = (err * scale).astype(BF16)
        out[...] = grad
        part[:, :latents] = contract(grad, tiles[...], 1, 0)
        part[:, latents:] = jnp.broadcast_to(loss, (loss.shape[0], BLK))


def second_kernel(out_g, out_k, act_g, act_k, second):
    latents = act_g.shape[1]
    for start in range(0, latents, 2 * BLK):
        columns = slice(start, start + 2 * BLK)
        second[:, columns] = contract(out_k[...], act_k[:, columns], 0, 0) + contract(
            out_g[...], act_g[:, columns], 0, 0
        )


def gate_kernel(parts, pre, live, spread, loss):
    latents = pre.shape[1]
    total = jnp.sum(parts[...], axis=0)
    grad = (jnp.where(pre[...] > 0, total[:, :latents], 0.0) * live[...]).astype(BF16)
    spread[...] = jnp.broadcast_to(grad[None], spread.shape)
    loss[...] = total[:, latents:]


def contribution_kernel(slots, ids, c_t, gp_g, gp_k, second, head, tail, stage, sems):
    half = gp_g.shape[0]
    cut = head.shape[1]
    copies = []
    for s in range(0, slots, 2):
        columns = slice(s * BLK, (s + 2) * BLK)
        total = (
            contract(c_t[:, :half], gp_g[:, columns], 1, 0)
            + contract(c_t[:, half:], gp_k[:, columns], 1, 0)
            + second[:, columns]
        ).astype(BF16)
        for i in range(s, s + 2):
            part = total[:, (i - s) * BLK : (i - s + 1) * BLK]
            tail[i] = part[cut:]
            stage[i] = part[:cut]
            copy = pltpu.make_async_copy(stage.at[i], head.at[ids[i] // 2], sems.at[i])
            copy.start()
            copies.append(copy)
    for copy in copies:
        copy.wait()


def combine_kernel(sources, places, head, tail, out, total):
    y = pl.program_id(0)
    cut = head.shape[2]
    total[...] = jnp.zeros_like(total)
    for x in range(sources):
        place = places[x, y]

        @pl.when(place >= 0)
        def _():
            b = place % 2
            total[b, :cut] += head[x, 0].astype(F32)
            total[b, cut:] += tail[x, place // 2].astype(F32)

    for b in range(2):
        out[0, :, b * BLK : (b + 1) * BLK] = total[b].astype(BF16)


def on_device(activations, weight, enc_bias, dec_bias, block_ids, counts):
    rows, width = activations.shape
    owners = lax.axis_size("latent")
    groups = lax.axis_size("dp")
    share = rows // groups
    chips = groups // 2
    half = rows // 2
    slots = block_ids.shape[1]
    latents = slots * BLK
    myself = lax.axis_index("latent")
    core = lax.axis_index("dp") % 2
    same_core = [[2 * z + c for z in range(chips)] for c in range(2)]
    swap = [(q, q ^ 1) for q in range(groups)]
    down = math.gcd(owners, 8) if owners > 8 else owners // 2
    across = owners // down
    same_x = [[x * down + y for y in range(down)] for x in range(across)]
    same_y = [[x * down + y for x in range(across)] for y in range(down)]
    my_x, my_y = myself // down, myself % down
    cut = width * 5 // 8

    def across_chips(array):
        return lax.all_to_all(array, "dp", 0, 0, tiled=True, axis_index_groups=same_core)

    def shape(dims, dtype):
        return jax.ShapeDtypeStruct(dims, dtype)

    column = lax.all_gather(weight, "latent", axis=0, axis_index_groups=same_x)

    ids = block_ids[0]
    note = jnp.concatenate([ids, counts])
    note = jnp.pad(note, (0, BLK - slots - 1))
    notes = lax.all_to_all(
        jnp.broadcast_to(note, (owners, 8, BLK)), "latent", 0, 0, tiled=True
    )[:, 0, :]
    row_notes = lax.dynamic_index_in_dim(
        notes.reshape(across, down, BLK), my_y, 1, keepdims=False
    )
    row_ids = row_notes[:, :slots]
    row_live = jnp.arange(slots)[None, :] < row_notes[:, slots : slots + 1]
    column_owners = my_x * down + jnp.arange(down)
    match = row_ids[:, None, :] // 2 == column_owners[None, :, None]
    upper = jnp.any(match & (row_ids % 2 == 1)[:, None, :], axis=2)
    code = jnp.arange(slots)[None, :] * 2 + row_ids % 2 + 1
    places = jnp.sum(jnp.where(match & row_live[:, None, :], code[:, None, :], 0), axis=2) - 1

    blocks = jnp.where(
        upper[:, :, None, None], column[None, :, :, BLK:], column[None, :, :, :BLK]
    )
    blocks = lax.all_to_all(
        blocks.reshape(owners, width, BLK), "latent", 0, 0, tiled=True, axis_index_groups=same_y
    )

    live = (jnp.arange(slots) < counts[0]).astype(F32)
    live_row = jnp.repeat(live, BLK)[None, :]
    bias_row = jnp.take(enc_bias.reshape(-1, BLK), ids, axis=0).reshape(1, latents)
    x_g, x_k, c_g, c_k, c_t = call(
        prepare_kernel,
        (shape((half, width), BF16),) * 4 + (shape((width, rows), BF16),),
        [SMEM_SPEC, VMEM_SPEC, VMEM_SPEC],
        (VMEM_SPEC,) * 5,
        flops=rows * width * 4,
        bytes_accessed=rows * width * 8,
    )(core[None], activations.reshape(chips, 2, share, width), dec_bias[None, :])

    matmul = 2 * half * width * latents
    give, keep, tiles = call(
        functools.partial(encode_kernel, slots),
        (shape((half, latents), F32), shape((half, latents), F32), shape((width, latents), BF16)),
        [SMEM_SPEC, VMEM_SPEC, VMEM_SPEC, ANY_SPEC],
        (VMEM_SPEC, VMEM_SPEC, VMEM_SPEC),
        flops=2 * matmul,
        bytes_accessed=4 * half * latents * 4,
        scratch=[pltpu.SemaphoreType.DMA((slots,))],
    )(ids, c_g, c_k, blocks)

    keep = keep + lax.ppermute(give, "dp", swap)
    parts = across_chips(keep.reshape(chips, share, latents))
    pre, spread = call(
        activate_kernel,
        (shape((share, latents), F32), shape((chips, share, latents), BF16)),
        [VMEM_SPEC] * 3,
        (VMEM_SPEC, VMEM_SPEC),
        bytes_accessed=half * latents * 6,
    )(parts, bias_row, live_row)
    act_k = across_chips(spread).reshape(half, latents)
    act_g = lax.ppermute(act_k, "dp", swap)

    scale = 2.0 / math.sqrt(rows * owners)
    give, keep, out_g, out_k = call(
        functools.partial(error_kernel, scale, 1.0 / (width * groups)),
        (
            shape((half, latents + BLK), F32),
            shape((half, latents + BLK), F32),
            shape((half, width), BF16),
            shape((half, width), BF16),
        ),
        [VMEM_SPEC] * 6,
        (VMEM_SPEC,) * 4,
        flops=4 * matmul,
        bytes_accessed=half * latents * 14,
    )(act_g, act_k, tiles, x_g, x_k, dec_bias[None, :])
    keep = keep + lax.ppermute(give, "dp", swap)
    parts = across_chips(keep.reshape(chips, share, latents + BLK))
    second = call(
        second_kernel,
        shape((width, latents), F32),
        [VMEM_SPEC] * 4,
        VMEM_SPEC,
        flops=2 * matmul,
        bytes_accessed=half * latents * 16,
    )(out_g, out_k, act_g, act_k)
    spread, loss = call(
        gate_kernel,
        (shape((chips, share, latents), BF16), shape((share, BLK), F32)),
        [VMEM_SPEC] * 3,
        (VMEM_SPEC, VMEM_SPEC),
        bytes_accessed=half * latents * 6,
    )(parts, pre, live_row)
    row_error = loss[:, 0]
    gp_k = across_chips(spread).reshape(half, latents)
    gp_g = lax.ppermute(gp_k, "dp", swap)

    head, tail = call(
        functools.partial(contribution_kernel, slots),
        (shape((owners, cut, BLK), BF16), shape((slots, width - cut, BLK), BF16)),
        [SMEM_SPEC] + [VMEM_SPEC] * 4,
        (HBM_SPEC, VMEM_SPEC),
        flops=2 * matmul,
        bytes_accessed=half * latents * 16,
        scratch=[pltpu.VMEM((slots, cut, BLK), BF16), pltpu.SemaphoreType.DMA((slots,))],
    )(ids, c_t, gp_g, gp_k, second)
    tail = lax.all_gather(tail, "latent", axis=0, axis_index_groups=same_y)
    head = lax.all_to_all(head, "latent", 0, 0, tiled=True, axis_index_groups=same_y)
    sums = pl.pallas_call(
        functools.partial(combine_kernel, across),
        grid=(down,),
        in_specs=[
            SMEM_SPEC,
            pl.BlockSpec((across, 1, cut, BLK), lambda y: (0, y, 0, 0)),
            VMEM_SPEC,
        ],
        out_specs=pl.BlockSpec((1, width, 2 * BLK), lambda y: (y, 0, 0)),
        out_shape=shape((down, width, 2 * BLK), BF16),
        scratch_shapes=[pltpu.VMEM((2, width, BLK), F32)],
        compiler_params=pltpu.CompilerParams(vmem_limit_bytes=VMEM_LIMIT),
        cost_estimate=pl.CostEstimate(
            flops=owners * width * BLK, bytes_accessed=owners * width * BLK * 2, transcendentals=0
        ),
    )(places, head.reshape(across, down, cut, BLK), tail)
    sums = lax.all_to_all(sums, "latent", 0, 0, tiled=True, axis_index_groups=same_x)
    weight_grad = jnp.sum(sums.astype(F32), axis=0)
    return (weight_grad, row_error)


def solution(mesh):
    placed = (P("latent", "dp"), P("dp", "latent"), P(), P("dp"), P("latent", None), P("latent"))
    return jax.shard_map(
        on_device,
        mesh=mesh,
        in_specs=placed,
        out_specs=(P("dp", "latent"), P(("latent", "dp"))),
        check_vma=False,
    )
```

```python
import functools
import math

import jax
import jax.numpy as jnp
from jax import lax
from jax.experimental import pallas as pl
from jax.experimental.pallas import tpu as pltpu
from jax.sharding import PartitionSpec as P

BLK = 128
BF16 = jnp.bfloat16
F32 = jnp.float32
VMEM_LIMIT = 40 * 1024 * 1024
SMEM_SPEC = pl.BlockSpec(memory_space=pltpu.SMEM)
VMEM_SPEC = pl.BlockSpec(memory_space=pltpu.VMEM)
ANY_SPEC = pl.BlockSpec(memory_space=pl.ANY)


def contract(a, b, dim_a, dim_b):
    return lax.dot_general(a, b, (((dim_a,), (dim_b,)), ((), ())), preferred_element_type=F32)


def call(kernel, out_shape, in_specs, out_specs, flops=0, bytes_accessed=0, scratch=(), **more):
    return pl.pallas_call(
        kernel,
        out_shape=out_shape,
        in_specs=in_specs,
        out_specs=out_specs,
        scratch_shapes=list(scratch),
        compiler_params=pltpu.CompilerParams(vmem_limit_bytes=VMEM_LIMIT),
        cost_estimate=pl.CostEstimate(
            flops=flops, bytes_accessed=bytes_accessed, transcendentals=0
        ),
        **more,
    )


def prepare_kernel(which, x, bias, x_g, x_k, c_g, c_k, c_t):
    half = x_g.shape[0]
    core = which[0]
    for i, (part, out) in enumerate(((x_g, c_g), (x_k, c_k))):
        rows = x[:, (1 - core) if i == 0 else core].reshape(part.shape)
        part[...] = rows
        centered = rows.astype(F32) - bias[...]
        out[...] = centered.astype(BF16)
        c_t[:, i * half : (i + 1) * half] = centered.T.astype(BF16)


def encode_kernel(slots, ids, give_x, keep_x, blocks, give, keep, tiles, sems):
    copies = []
    for s in range(slots):
        copy = pltpu.make_async_copy(
            blocks.at[ids[s] // 2], tiles.at[:, pl.ds(s * BLK, BLK)], sems.at[s]
        )
        copy.start()
        copies.append(copy)
    for s in range(0, slots, 2):
        for copy in copies[s : s + 2]:
            copy.wait()
        columns = slice(s * BLK, (s + 2) * BLK)
        part = tiles[:, columns]
        give[:, columns] = contract(give_x[...], part, 1, 0)
        keep[:, columns] = contract(keep_x[...], part, 1, 0)


def activate_kernel(parts, bias, live, pre, spread):
    total = jnp.sum(parts[...], axis=0) + bias[...]
    pre[...] = total
    act = (jnp.maximum(total, 0.0) * live[...]).astype(BF16)
    spread[...] = jnp.broadcast_to(act[None], spread.shape)


def error_kernel(scale, loss_scale, act_g, act_k, tiles, x_g, x_k, bias, give, keep, out_g, out_k):
    latents = tiles.shape[1]
    for act, x, part, out in ((act_g, x_g, give, out_g), (act_k, x_k, keep, out_k)):
        err = contract(act[...], tiles[...], 1, 1) + bias[...] - x[...].astype(F32)
        loss = jnp.sum(err * err, axis=1, keepdims=True) * loss_scale
        grad = (err * scale).astype(BF16)
        out[...] = grad
        latent_grad = contract(grad, tiles[...], 1, 0)
        part[:, :latents] = latent_grad
        top = jnp.max(jnp.abs(latent_grad), axis=1, keepdims=True)
        lane = lax.broadcasted_iota(jnp.int32, (loss.shape[0], BLK), 1)
        part[:, latents:] = jnp.where(lane == 0, loss, top)


def second_kernel(out_g, out_k, act_g, act_k, second):
    latents = act_g.shape[1]
    for start in range(0, latents, 2 * BLK):
        columns = slice(start, start + 2 * BLK)
        second[:, columns] = contract(out_k[...], act_k[:, columns], 0, 0) + contract(
            out_g[...], act_g[:, columns], 0, 0
        )


def power_above(x):
    return jnp.ceil(jnp.log2(jnp.maximum(x, 1e-30)))


def pack_kernel(keep, got, out):
    latents = out.shape[1] - BLK
    total = keep[...] + got[...]
    loss, top = total[:, latents : latents + 1], total[:, latents + 1 : latents + 2]
    top = power_above(top)
    power = power_above(loss)
    scaled = loss * jnp.exp2(-power)
    first = scaled.astype(BF16).astype(F32)
    rest = (scaled - first) * 256.0
    lane = lax.broadcasted_iota(jnp.int32, (total.shape[0], BLK), 1)
    out[:, :latents] = total[:, :latents] * jnp.exp2(14.0 - top)
    out[:, latents:] = jnp.where(
        lane == 0, top, jnp.where(lane == 1, power, jnp.where(lane == 2, first, rest))
    )


def gate_kernel(parts, pre, live, spread, loss):
    chips, _, width = parts.shape
    latents = width - BLK
    total = jnp.zeros(pre.shape, F32)
    error = jnp.zeros(loss.shape, F32)
    for z in range(chips):
        extra = parts[z, :, latents:]
        total += parts[z, :, :latents] * jnp.exp2(extra[:, :1] - 14.0)
        row = (extra[:, 2:3] + extra[:, 3:4] * (1.0 / 256.0)) * jnp.exp2(extra[:, 1:2])
        error += jnp.broadcast_to(row, loss.shape)
    grad = (jnp.where(pre[...] > 0, total, 0.0) * live[...]).astype(BF16)
    spread[...] = jnp.broadcast_to(grad[None], spread.shape)
    loss[...] = error


def contribution_kernel(slots, c_t, gp_g, gp_k, second, low, high):
    half = gp_g.shape[0]
    cut = low.shape[1]
    for s in range(0, slots, 2):
        columns = slice(s * BLK, (s + 2) * BLK)
        total = (
            contract(c_t[:, :half], gp_g[:, columns], 1, 0)
            + contract(c_t[:, half:], gp_k[:, columns], 1, 0)
            + second[:, columns]
        ).astype(BF16)
        for i in range(s, s + 2):
            part = total[:, (i - s) * BLK : (i - s + 1) * BLK]
            low[i] = part[:cut]
            high[i] = part[cut:]


def combine_kernel(places, own, after, far_a, far_b, before, out, total):
    y = pl.program_id(0)
    few = far_a.shape[0]
    total[...] = jnp.zeros_like(total)
    for x in range(4):
        place = places[x, y]
        b = place % 2
        slot = place // 2
        if x == 2:

            @pl.when((place >= 0) & (slot < few))
            def _():
                total[b] += far_a[slot].astype(F32)

            @pl.when(slot >= few)
            def _():
                total[b] += far_b[slot - few].astype(F32)
        else:
            source = (own, after, None, before)[x]

            @pl.when(place >= 0)
            def _():
                total[b] += source[slot].astype(F32)

    for b in range(2):
        out[0, :, b * BLK : (b + 1) * BLK] = total[b].astype(BF16)


def on_device(activations, weight, enc_bias, dec_bias, block_ids, counts):
    rows, width = activations.shape
    owners = lax.axis_size("latent")
    groups = lax.axis_size("dp")
    share = rows // groups
    chips = groups // 2
    half = rows // 2
    slots = block_ids.shape[1]
    latents = slots * BLK
    myself = lax.axis_index("latent")
    core = lax.axis_index("dp") % 2
    same_core = [[2 * z + c for z in range(chips)] for c in range(2)]
    swap = [(q, q ^ 1) for q in range(groups)]
    across = 4
    down = owners // across
    same_x = [[x * down + y for y in range(down)] for x in range(across)]
    same_y = [[x * down + y for x in range(across)] for y in range(down)]
    my_x, my_y = myself // down, myself % down
    cut = width // 2
    next_x = [(j, (j + down) % owners) for j in range(owners)]
    last_x = [(j, (j - down) % owners) for j in range(owners)]

    def across_chips(array):
        return lax.all_to_all(array, "dp", 0, 0, tiled=True, axis_index_groups=same_core)

    def shape(dims, dtype):
        return jax.ShapeDtypeStruct(dims, dtype)

    column = lax.all_gather(weight, "latent", axis=0, axis_index_groups=same_x)

    ids = block_ids[0]
    note = jnp.concatenate([ids, counts])
    note = jnp.pad(note, (0, BLK - slots - 1))
    notes = lax.all_to_all(
        jnp.broadcast_to(note, (owners, 8, BLK)), "latent", 0, 0, tiled=True
    )[:, 0, :]
    row_notes = lax.dynamic_index_in_dim(
        notes.reshape(across, down, BLK), my_y, 1, keepdims=False
    )
    row_ids = row_notes[:, :slots]
    row_live = jnp.arange(slots)[None, :] < row_notes[:, slots : slots + 1]
    column_owners = my_x * down + jnp.arange(down)
    match = row_ids[:, None, :] // 2 == column_owners[None, :, None]
    upper = jnp.any(match & (row_ids % 2 == 1)[:, None, :], axis=2)
    code = jnp.arange(slots)[None, :] * 2 + row_ids % 2 + 1
    places = jnp.sum(jnp.where(match & row_live[:, None, :], code[:, None, :], 0), axis=2) - 1
    places = jnp.roll(places, -my_x, axis=0)

    blocks = jnp.where(
        upper[:, :, None, None], column[None, :, :, BLK:], column[None, :, :, :BLK]
    )
    blocks = lax.all_to_all(
        blocks.reshape(owners, width, BLK), "latent", 0, 0, tiled=True, axis_index_groups=same_y
    )

    live = (jnp.arange(slots) < counts[0]).astype(F32)
    live_row = jnp.repeat(live, BLK)[None, :]
    bias_row = jnp.take(enc_bias.reshape(-1, BLK), ids, axis=0).reshape(1, latents)
    x_g, x_k, c_g, c_k, c_t = call(
        prepare_kernel,
        (shape((half, width), BF16),) * 4 + (shape((width, rows), BF16),),
        [SMEM_SPEC, VMEM_SPEC, VMEM_SPEC],
        (VMEM_SPEC,) * 5,
        flops=rows * width * 4,
        bytes_accessed=rows * width * 8,
    )(core[None], activations.reshape(chips, 2, share, width), dec_bias[None, :])

    matmul = 2 * half * width * latents
    give, keep, tiles = call(
        functools.partial(encode_kernel, slots),
        (shape((half, latents), F32), shape((half, latents), F32), shape((width, latents), BF16)),
        [SMEM_SPEC, VMEM_SPEC, VMEM_SPEC, ANY_SPEC],
        (VMEM_SPEC, VMEM_SPEC, VMEM_SPEC),
        flops=2 * matmul,
        bytes_accessed=4 * half * latents * 4,
        scratch=[pltpu.SemaphoreType.DMA((slots,))],
    )(ids, c_g, c_k, blocks)

    keep = keep + lax.ppermute(give, "dp", swap)
    parts = across_chips(keep.reshape(chips, share, latents))
    pre, spread = call(
        activate_kernel,
        (shape((share, latents), F32), shape((chips, share, latents), BF16)),
        [VMEM_SPEC] * 3,
        (VMEM_SPEC, VMEM_SPEC),
        bytes_accessed=half * latents * 6,
    )(parts, bias_row, live_row)
    act_k = across_chips(spread).reshape(half, latents)
    act_g = lax.ppermute(act_k, "dp", swap)

    scale = 2.0 / math.sqrt(rows * owners)
    give, keep, out_g, out_k = call(
        functools.partial(error_kernel, scale, 1.0 / (width * groups)),
        (
            shape((half, latents + BLK), F32),
            shape((half, latents + BLK), F32),
            shape((half, width), BF16),
            shape((half, width), BF16),
        ),
        [VMEM_SPEC] * 6,
        (VMEM_SPEC,) * 4,
        flops=4 * matmul,
        bytes_accessed=half * latents * 14,
    )(act_g, act_k, tiles, x_g, x_k, dec_bias[None, :])
    packed = call(
        pack_kernel,
        shape((half, latents + BLK), F32),
        [VMEM_SPEC] * 2,
        VMEM_SPEC,
        bytes_accessed=half * latents * 12,
    )(keep, lax.ppermute(give, "dp", swap))
    parts = across_chips(packed.astype(jnp.float16).reshape(chips, share, latents + BLK))
    second = call(
        second_kernel,
        shape((width, latents), F32),
        [VMEM_SPEC] * 4,
        VMEM_SPEC,
        flops=2 * matmul,
        bytes_accessed=half * latents * 16,
    )(out_g, out_k, act_g, act_k)
    spread, loss = call(
        gate_kernel,
        (shape((chips, share, latents), BF16), shape((share, BLK), F32)),
        [VMEM_SPEC] * 3,
        (VMEM_SPEC, VMEM_SPEC),
        bytes_accessed=half * latents * 6,
    )(parts.astype(F32), pre, live_row)
    row_error = loss[:, 0]
    gp_k = across_chips(spread).reshape(half, latents)
    gp_g = lax.ppermute(gp_k, "dp", swap)

    halves = call(
        functools.partial(contribution_kernel, slots),
        (shape((slots, cut, BLK), BF16), shape((slots, width - cut, BLK), BF16)),
        [VMEM_SPEC] * 4,
        (VMEM_SPEC, VMEM_SPEC),
        flops=2 * matmul,
        bytes_accessed=half * latents * 16,
    )(c_t, gp_g, gp_k, second)

    few = slots // 2
    grads = []
    for part in halves:
        before = lax.ppermute(part, "latent", next_x)
        after = lax.ppermute(part, "latent", last_x)
        far_a = lax.ppermute(after[:few], "latent", last_x)
        far_b = lax.ppermute(before[few:], "latent", next_x)
        features = part.shape[1]
        sums = pl.pallas_call(
            combine_kernel,
            grid=(down,),
            in_specs=[SMEM_SPEC] + [VMEM_SPEC] * 5,
            out_specs=pl.BlockSpec((1, features, 2 * BLK), lambda y: (y, 0, 0)),
            out_shape=shape((down, features, 2 * BLK), BF16),
            scratch_shapes=[pltpu.VMEM((2, features, BLK), F32)],
            compiler_params=pltpu.CompilerParams(vmem_limit_bytes=VMEM_LIMIT),
            cost_estimate=pl.CostEstimate(
                flops=owners * features * BLK,
                bytes_accessed=owners * features * BLK * 2,
                transcendentals=0,
            ),
        )(places, part, after, far_a, far_b, before)
        sums = lax.all_to_all(sums, "latent", 0, 0, tiled=True, axis_index_groups=same_x)
        grads.append(jnp.sum(sums.astype(F32), axis=0))
    weight_grad = jnp.concatenate(grads, axis=0)
    return (weight_grad, row_error)


def solution(mesh):
    placed = (P("latent", "dp"), P("dp", "latent"), P(), P("dp"), P("latent", None), P("latent"))
    return jax.shard_map(
        on_device,
        mesh=mesh,
        in_specs=placed,
        out_specs=(P("dp", "latent"), P(("latent", "dp"))),
        check_vma=False,
    )
```

```python
import functools
import math

import jax
import jax.numpy as jnp
from jax import lax
from jax.experimental import pallas as pl
from jax.experimental.pallas import tpu as pltpu
from jax.sharding import PartitionSpec as P

BLK = 128
BF16 = jnp.bfloat16
F32 = jnp.float32
VMEM_LIMIT = 20 * 1024 * 1024
SMEM_SPEC = pl.BlockSpec(memory_space=pltpu.SMEM)
VMEM_SPEC = pl.BlockSpec(memory_space=pltpu.VMEM)
ANY_SPEC = pl.BlockSpec(memory_space=pl.ANY)


def contract(a, b, dim_a, dim_b):
    return lax.dot_general(a, b, (((dim_a,), (dim_b,)), ((), ())), preferred_element_type=F32)


def call(kernel, out_shape, in_specs, out_specs, flops=0, bytes_accessed=0, scratch=(), **more):
    return pl.pallas_call(
        kernel,
        out_shape=out_shape,
        in_specs=in_specs,
        out_specs=out_specs,
        scratch_shapes=list(scratch),
        compiler_params=pltpu.CompilerParams(vmem_limit_bytes=VMEM_LIMIT),
        cost_estimate=pl.CostEstimate(
            flops=flops, bytes_accessed=bytes_accessed, transcendentals=0
        ),
        **more,
    )


def prepare_kernel(which, x, bias, x_g, x_k, c_g, c_k, c_t):
    half = x_g.shape[0]
    core = which[0]
    for i, (part, out) in enumerate(((x_g, c_g), (x_k, c_k))):
        rows = x[:, (1 - core) if i == 0 else core].reshape(part.shape)
        part[...] = rows
        centered = rows.astype(F32) - bias[...]
        out[...] = centered.astype(BF16)
        c_t[:, i * half : (i + 1) * half] = centered.T.astype(BF16)


def encode_kernel(slots, ids, rows, blocks, out, tiles, raw, sems):
    side = BLK // 2
    middle = slots * side
    copies = []
    for s in range(slots):
        copy = pltpu.make_async_copy(blocks.at[ids[s] // 2], raw.at[s], sems.at[s])
        copy.start()
        copies.append(copy)
    for s in range(0, slots, 2):
        copies[s].wait()
        copies[s + 1].wait()
        one, two = raw[s], raw[s + 1]
        start = s * side
        tiles[:, start : start + BLK] = jnp.concatenate([one[:, :side], two[:, :side]], axis=1)
        tiles[:, middle + start : middle + start + BLK] = jnp.concatenate(
            [one[:, side:], two[:, side:]], axis=1
        )
    for start in range(0, 2 * middle, 2 * BLK):
        columns = slice(start, start + 2 * BLK)
        out[:, columns] = contract(rows[...], tiles[:, columns], 1, 0)


def encode_rest_kernel(rows, tiles, got, out):
    for start in range(0, out.shape[1], 2 * BLK):
        columns = slice(start, start + 2 * BLK)
        out[:, columns] = contract(rows[...], tiles[:, columns], 1, 0) + got[:, columns]


def activate_kernel(parts, bias, live, pre, spread):
    total = jnp.sum(parts[...], axis=0) + bias[...]
    pre[...] = total
    act = (jnp.maximum(total, 0.0) * live[...]).astype(BF16)
    spread[...] = jnp.broadcast_to(act[None], spread.shape)


def error_kernel(scale, loss_scale, act, tiles, x, bias, part, out):
    latents = tiles.shape[1]
    err = contract(act[...], tiles[...], 1, 1) + bias[...] - x[...].astype(F32)
    loss = jnp.sum(err * err, axis=1, keepdims=True) * loss_scale
    grad = (err * scale).astype(BF16)
    out[...] = grad
    latent_grad = contract(grad, tiles[...], 1, 0)
    part[:, :latents] = latent_grad
    top = jnp.max(jnp.abs(latent_grad), axis=1, keepdims=True)
    lane = lax.broadcasted_iota(jnp.int32, (loss.shape[0], BLK), 1)
    part[:, latents:] = jnp.where(lane == 0, loss, top)


def second_kernel(out_g, out_k, act_g, act_k, first_half, second_half):
    middle = first_half.shape[1]
    for i, second in enumerate((first_half, second_half)):
        for start in range(0, middle, 2 * BLK):
            columns = slice(i * middle + start, i * middle + start + 2 * BLK)
            second[:, start : start + 2 * BLK] = contract(
                out_k[...], act_k[:, columns], 0, 0
            ) + contract(out_g[...], act_g[:, columns], 0, 0)


def power_above(x):
    return jnp.ceil(jnp.log2(jnp.maximum(x, 1e-30)))


def pack_kernel(keep, got, out):
    middle = out.shape[1] - BLK
    extra = keep[:, 2 * middle :] + got[:, 2 * middle :]
    loss, top = extra[:, :1], power_above(extra[:, 1:2])
    power = power_above(loss)
    scaled = loss * jnp.exp2(-power)
    first = scaled.astype(BF16).astype(F32)
    rest = (scaled - first) * 256.0
    lane = lax.broadcasted_iota(jnp.int32, extra.shape, 1)
    out[:, :middle] = (keep[:, :middle] + got[:, :middle]) * jnp.exp2(14.0 - top)
    out[:, middle:] = jnp.where(
        lane == 0, top, jnp.where(lane == 1, power, jnp.where(lane == 2, first, rest))
    )


def pack_rest_kernel(keep, got, earlier, out):
    middle = out.shape[1]
    extra = keep[:, 2 * middle :] + got[:, 2 * middle :]
    top = power_above(extra[:, 1:2])
    out[...] = (keep[:, middle : 2 * middle] + got[:, middle : 2 * middle]) * jnp.exp2(14.0 - top)


def gate_kernel(start, parts, extras, pre, live, spread, loss):
    chips, _, middle = spread.shape
    shape = (pre.shape[0], middle)
    total = jnp.zeros(shape, F32)
    error = jnp.zeros(loss.shape, F32)
    for z in range(chips):
        extra = extras[z, :, middle:]
        total += parts[z, :, :middle] * jnp.exp2(extra[:, :1] - 14.0)
        row = (extra[:, 2:3] + extra[:, 3:4] * (1.0 / 256.0)) * jnp.exp2(extra[:, 1:2])
        error += jnp.broadcast_to(row, loss.shape)
    columns = slice(start, start + middle)
    grad = (jnp.where(pre[:, columns] > 0, total, 0.0) * live[:, columns]).astype(BF16)
    spread[...] = jnp.broadcast_to(grad[None], spread.shape)
    loss[...] = error


def contribution_kernel(c_t, gp_g, gp_k, second, out):
    half = gp_g.shape[0]
    for i in range(0, out.shape[0], 2):
        columns = slice(i * BLK, (i + 2) * BLK)
        total = (
            contract(c_t[:, :half], gp_g[:, columns], 1, 0)
            + contract(c_t[:, half:], gp_k[:, columns], 1, 0)
            + second[:, columns]
        ).astype(BF16)
        out[i] = total[:, :BLK]
        out[i + 1] = total[:, BLK:]


def combine_kernel(places, own, after, far_a, far_b, before, out, total):
    y = pl.program_id(0)
    few = far_a.shape[0]
    side = BLK // 2
    found = jnp.maximum(
        jnp.maximum(places[0, y], places[1, y]), jnp.maximum(places[2, y], places[3, y])
    )

    @pl.when(found < 0)
    def _():
        out[...] = jnp.zeros_like(out)

    @pl.when(found >= 0)
    def _():
        total[...] = jnp.zeros_like(total)
        lower = lax.broadcasted_iota(jnp.int32, total.shape, 1) < side

        def add(source, pair, b, odd):
            value = source[pair].astype(F32)

            @pl.when(b == odd)
            def _():
                total[...] += jnp.where(lower == (b == 0), value, 0.0)

            @pl.when(b != odd)
            def _():
                total[...] += jnp.where(lower == (b == 0), pltpu.roll(value, side, 1), 0.0)

        for x in range(4):
            place = places[x, y]
            b, slot = place % 2, place // 2
            pair, odd = slot // 2, slot % 2
            if x == 2:

                @pl.when((place >= 0) & (pair < few))
                def _():
                    add(far_a, pair, b, odd)

                @pl.when((place >= 0) & (pair >= few))
                def _():
                    add(far_b, pair - few, b, odd)
            else:
                source = (own, after, None, before)[x]

                @pl.when(place >= 0)
                def _():
                    add(source, pair, b, odd)

        out[0] = total[...].astype(BF16)


def finish_kernel(first, second, out):
    side = BLK // 2
    total = jnp.sum(second[...].astype(F32), axis=0)
    for b in range(2):
        columns = slice(b * side, (b + 1) * side)
        out[:, b * BLK : (b + 1) * BLK] = jnp.concatenate(
            [first[:, columns], total[:, columns]], axis=1
        )


def on_device(activations, weight, enc_bias, dec_bias, block_ids, counts):
    rows, width = activations.shape
    owners = lax.axis_size("latent")
    groups = lax.axis_size("dp")
    share = rows // groups
    chips = groups // 2
    half = rows // 2
    slots = block_ids.shape[1]
    latents = slots * BLK
    myself = lax.axis_index("latent")
    core = lax.axis_index("dp") % 2
    same_core = [[2 * z + c for z in range(chips)] for c in range(2)]
    swap = [(q, q ^ 1) for q in range(groups)]
    across = 4
    down = owners // across
    same_x = [[x * down + y for y in range(down)] for x in range(across)]
    same_y = [[x * down + y for x in range(across)] for y in range(down)]
    my_x, my_y = myself // down, myself % down
    next_x = [(j, (j + down) % owners) for j in range(owners)]
    last_x = [(j, (j - down) % owners) for j in range(owners)]

    def across_chips(array):
        return lax.all_to_all(array, "dp", 0, 0, tiled=True, axis_index_groups=same_core)

    def shape(dims, dtype):
        return jax.ShapeDtypeStruct(dims, dtype)

    column = lax.all_gather(weight, "latent", axis=0, axis_index_groups=same_x)

    ids = block_ids[0]
    note = jnp.concatenate([ids, counts])
    note = jnp.pad(note, (0, BLK - slots - 1))
    notes = lax.all_to_all(
        jnp.broadcast_to(note, (owners, 8, BLK)), "latent", 0, 0, tiled=True
    )[:, 0, :]
    row_notes = lax.dynamic_index_in_dim(
        notes.reshape(across, down, BLK), my_y, 1, keepdims=False
    )
    row_ids = row_notes[:, :slots]
    row_live = jnp.arange(slots)[None, :] < row_notes[:, slots : slots + 1]
    column_owners = my_x * down + jnp.arange(down)
    match = row_ids[:, None, :] // 2 == column_owners[None, :, None]
    upper = jnp.any(match & (row_ids % 2 == 1)[:, None, :], axis=2)
    code = jnp.arange(slots)[None, :] * 2 + row_ids % 2 + 1
    places = jnp.sum(jnp.where(match & row_live[:, None, :], code[:, None, :], 0), axis=2) - 1
    places = jnp.roll(places, -my_x, axis=0)

    blocks = jnp.where(
        upper[:, :, None, None], column[None, :, :, BLK:], column[None, :, :, :BLK]
    )
    blocks = lax.all_to_all(
        blocks.reshape(owners, width, BLK), "latent", 0, 0, tiled=True, axis_index_groups=same_y
    )

    live = (jnp.arange(slots) < counts[0]).astype(F32)
    live_row = jnp.tile(jnp.repeat(live, BLK // 2), 2)[None, :]
    bias_row = jnp.take(enc_bias.reshape(-1, BLK), ids, axis=0)
    bias_row = bias_row.reshape(slots, 2, BLK // 2).transpose(1, 0, 2).reshape(1, latents)
    x_g, x_k, c_g, c_k, c_t = call(
        prepare_kernel,
        (shape((half, width), BF16),) * 4 + (shape((width, rows), BF16),),
        [SMEM_SPEC, VMEM_SPEC, VMEM_SPEC],
        (VMEM_SPEC,) * 5,
        flops=rows * width * 4,
        bytes_accessed=rows * width * 8,
    )(core[None], activations.reshape(chips, 2, share, width), dec_bias[None, :])

    matmul = 2 * half * width * latents
    middle = latents // 2
    give, tiles = call(
        functools.partial(encode_kernel, slots),
        (shape((half, latents), F32), shape((width, latents), BF16)),
        [SMEM_SPEC, VMEM_SPEC, ANY_SPEC],
        (VMEM_SPEC, VMEM_SPEC),
        flops=matmul,
        bytes_accessed=4 * half * latents * 3,
        scratch=[pltpu.VMEM((slots, width, BLK), BF16), pltpu.SemaphoreType.DMA((slots,))],
    )(ids, c_g, blocks)
    keep = call(
        encode_rest_kernel,
        shape((half, latents), F32),
        [VMEM_SPEC] * 3,
        VMEM_SPEC,
        flops=matmul,
        bytes_accessed=4 * half * latents * 3,
    )(c_k, tiles, lax.ppermute(give, "dp", swap))
    parts = across_chips(keep.reshape(chips, share, latents))
    pre, spread = call(
        activate_kernel,
        (shape((share, latents), F32), shape((chips, share, latents), BF16)),
        [VMEM_SPEC] * 3,
        (VMEM_SPEC, VMEM_SPEC),
        bytes_accessed=half * latents * 6,
    )(parts, bias_row, live_row)
    act_k = across_chips(spread).reshape(half, latents)
    act_g = lax.ppermute(act_k, "dp", swap)

    scale = 2.0 / math.sqrt(rows * owners)
    give, keep = (
        call(
            functools.partial(error_kernel, scale, 1.0 / (width * groups)),
            (shape((half, latents + BLK), F32), shape((half, width), BF16)),
            [VMEM_SPEC] * 4,
            (VMEM_SPEC,) * 2,
            flops=2 * matmul,
            bytes_accessed=half * latents * 7,
        )(act, tiles, x, dec_bias[None, :])
        for act, x in ((act_g, x_g), (act_k, x_k))
    )
    (give, out_g), (keep, out_k) = give, keep
    got = lax.ppermute(give, "dp", swap)
    second = call(
        second_kernel,
        (shape((width, middle), F32),) * 2,
        [VMEM_SPEC] * 4,
        (VMEM_SPEC,) * 2,
        flops=2 * matmul,
        bytes_accessed=half * latents * 16,
    )(out_g, out_k, act_g, act_k)

    parts = []
    extras = None
    for i in range(2):
        if i == 0:
            packed = call(
                pack_kernel,
                shape((half, middle + BLK), F32),
                [VMEM_SPEC] * 2,
                VMEM_SPEC,
                bytes_accessed=half * latents * 6,
            )(keep, got)
        else:
            packed = call(
                pack_rest_kernel,
                shape((half, middle), F32),
                [VMEM_SPEC] * 2 + [ANY_SPEC],
                VMEM_SPEC,
                bytes_accessed=half * latents * 6,
            )(keep, got, gp_k)
        sums = across_chips(packed.astype(jnp.float16).reshape(chips, share, -1)).astype(F32)
        extras = sums if extras is None else extras
        spread, loss = call(
            functools.partial(gate_kernel, i * middle),
            (shape((chips, share, middle), BF16), shape((share, BLK), F32)),
            [VMEM_SPEC] * 4,
            (VMEM_SPEC, VMEM_SPEC),
            bytes_accessed=half * latents * 3,
        )(sums, extras, pre, live_row)
        if i == 0:
            row_error = loss[:, 0]
        gp_k = across_chips(spread).reshape(half, middle)
        gp_g = lax.ppermute(gp_k, "dp", swap)
        parts.append(
            call(
                contribution_kernel,
                shape((slots // 2, width, BLK), BF16),
                [VMEM_SPEC] * 4,
                VMEM_SPEC,
                flops=matmul,
                bytes_accessed=half * latents * 8,
            )(c_t, gp_g, gp_k, second[i])
        )

    few = slots // 4
    grads = []
    for part in parts:
        before = lax.ppermute(part, "latent", next_x)
        after = lax.ppermute(part, "latent", last_x)
        far_a = lax.ppermute(after[:few], "latent", last_x)
        far_b = lax.ppermute(before[few:], "latent", next_x)
        sums = pl.pallas_call(
            combine_kernel,
            grid=(down,),
            in_specs=[SMEM_SPEC] + [VMEM_SPEC] * 5,
            out_specs=pl.BlockSpec((1, width, BLK), lambda y: (y, 0, 0)),
            out_shape=shape((down, width, BLK), BF16),
            scratch_shapes=[pltpu.VMEM((width, BLK), F32)],
            compiler_params=pltpu.CompilerParams(vmem_limit_bytes=VMEM_LIMIT),
            cost_estimate=pl.CostEstimate(
                flops=owners * width * BLK // 2,
                bytes_accessed=owners * width * BLK,
                transcendentals=0,
            ),
        )(places, part, after, far_a, far_b, before)
        grads.append(lax.all_to_all(sums, "latent", 0, 0, tiled=True, axis_index_groups=same_x))
    weight_grad = call(
        finish_kernel,
        shape((width, 2 * BLK), F32),
        [VMEM_SPEC] * 2,
        VMEM_SPEC,
        bytes_accessed=width * BLK * 8 * 4,
    )(jnp.sum(grads[0].astype(F32), axis=0), grads[1])
    return (weight_grad, row_error)


def solution(mesh):
    placed = (P("latent", "dp"), P("dp", "latent"), P(), P("dp"), P("latent", None), P("latent"))
    return jax.shard_map(
        on_device,
        mesh=mesh,
        in_specs=placed,
        out_specs=(P("dp", "latent"), P(("latent", "dp"))),
        check_vma=False,
    )
```

```python
import functools
import math

import jax
import jax.numpy as jnp
from jax import lax
from jax.experimental import pallas as pl
from jax.experimental.pallas import tpu as pltpu
from jax.sharding import PartitionSpec as P

BLK = 128
BF16 = jnp.bfloat16
F32 = jnp.float32
VMEM_LIMIT = 20 * 1024 * 1024
SMEM_SPEC = pl.BlockSpec(memory_space=pltpu.SMEM)
VMEM_SPEC = pl.BlockSpec(memory_space=pltpu.VMEM)
ANY_SPEC = pl.BlockSpec(memory_space=pl.ANY)


def contract(a, b, dim_a, dim_b):
    return lax.dot_general(a, b, (((dim_a,), (dim_b,)), ((), ())), preferred_element_type=F32)


def call(kernel, out_shape, in_specs, out_specs, flops=0, bytes_accessed=0, scratch=(), **more):
    return pl.pallas_call(
        kernel,
        out_shape=out_shape,
        in_specs=in_specs,
        out_specs=out_specs,
        scratch_shapes=list(scratch),
        compiler_params=pltpu.CompilerParams(vmem_limit_bytes=VMEM_LIMIT),
        cost_estimate=pl.CostEstimate(
            flops=flops, bytes_accessed=bytes_accessed, transcendentals=0
        ),
        **more,
    )


def prepare_kernel(which, x, bias, x_g, x_k, c_g, c_k, c_t):
    half = x_g.shape[0]
    core = which[0]
    for i, (part, out) in enumerate(((x_g, c_g), (x_k, c_k))):
        rows = x[:, (1 - core) if i == 0 else core].reshape(part.shape)
        part[...] = rows
        centered = rows.astype(F32) - bias[...]
        out[...] = centered.astype(BF16)
        c_t[:, i * half : (i + 1) * half] = centered.T.astype(BF16)


def fetch_kernel(slots, ids, blocks, tiles, sems):
    copies = []
    for s in range(slots):
        copy = pltpu.make_async_copy(
            blocks.at[ids[s] // 2], tiles.at[:, pl.ds(s * BLK, BLK)], sems.at[s]
        )
        copy.start()
        copies.append(copy)
    for copy in copies:
        copy.wait()


def encode_kernel(rows, tiles, out):
    for start in range(0, out.shape[1], 2 * BLK):
        columns = slice(start, start + 2 * BLK)
        out[:, columns] = contract(rows[...], tiles[:, columns], 1, 0)


def encode_rest_kernel(rows, tiles, part, out):
    for start in range(0, out.shape[1], 2 * BLK):
        columns = slice(start, start + 2 * BLK)
        out[:, columns] = contract(rows[...], tiles[:, columns], 1, 0) + part[:, columns]


def activate_kernel(parts, bias, live, pre, spread):
    total = jnp.sum(parts[...], axis=0) + bias[...]
    pre[...] = total
    act = (jnp.maximum(total, 0.0) * live[...]).astype(BF16)
    spread[...] = jnp.broadcast_to(act[None], spread.shape)


def power_above(x):
    return jnp.ceil(jnp.log2(jnp.maximum(x, 1e-30)))


def error_kernel(scale, loss_scale, act, tiles, tiles_o, x, x_o, bias, bias_o, out, grad_out, grad_out_o):
    latents = tiles.shape[1]
    loss = 0.0
    grads = []
    for w, rows, b, g in ((tiles, x, bias, grad_out), (tiles_o, x_o, bias_o, grad_out_o)):
        err = contract(act[...], w[...], 1, 1) + b[...] - rows[...].astype(F32)
        loss += jnp.sum(err * err, axis=1, keepdims=True) * loss_scale
        grad = (err * scale).astype(BF16)
        g[...] = grad
        grads.append(grad)
    total = contract(grads[0], tiles[...], 1, 0) + contract(grads[1], tiles_o[...], 1, 0)
    top = power_above(jnp.max(jnp.abs(total), axis=1, keepdims=True))
    power = power_above(loss)
    scaled = loss * jnp.exp2(-power)
    first = scaled.astype(BF16).astype(F32)
    rest = (scaled - first) * 256.0
    lane = lax.broadcasted_iota(jnp.int32, (total.shape[0], BLK), 1)
    out[:, :latents] = total * jnp.exp2(14.0 - top)
    out[:, latents:] = jnp.where(
        lane == 0, top, jnp.where(lane == 1, power, jnp.where(lane == 2, first, rest))
    )


def second_kernel(out_g, out_k, act_g, act_k, second):
    latents = act_g.shape[1]
    for start in range(0, latents, 2 * BLK):
        columns = slice(start, start + 2 * BLK)
        second[:, columns] = contract(out_k[...], act_k[:, columns], 0, 0) + contract(
            out_g[...], act_g[:, columns], 0, 0
        )


def gate_kernel(parts, pre, live, spread, loss):
    chips, _, width = parts.shape
    latents = width - BLK
    total = jnp.zeros(pre.shape, F32)
    error = jnp.zeros(loss.shape, F32)
    for z in range(chips):
        extra = parts[z, :, latents:]
        total += parts[z, :, :latents] * jnp.exp2(extra[:, :1] - 14.0)
        row = (extra[:, 2:3] + extra[:, 3:4] * (1.0 / 256.0)) * jnp.exp2(extra[:, 1:2])
        error += jnp.broadcast_to(row, loss.shape)
    grad = (jnp.where(pre[...] > 0, total, 0.0) * live[...]).astype(BF16)
    spread[...] = jnp.broadcast_to(grad[None], spread.shape)
    loss[...] = error


def contribution_kernel(slots, c_t, gp_g, gp_k, second, low, high):
    half = gp_g.shape[0]
    cut = low.shape[1]
    for s in range(0, slots, 2):
        columns = slice(s * BLK, (s + 2) * BLK)
        total = (
            contract(c_t[:, :half], gp_g[:, columns], 1, 0)
            + contract(c_t[:, half:], gp_k[:, columns], 1, 0)
            + second[:, columns]
        ).astype(BF16)
        for i in range(s, s + 2):
            part = total[:, (i - s) * BLK : (i - s + 1) * BLK]
            low[i] = part[:cut]
            high[i] = part[cut:]


def combine_kernel(places, own, after, far_a, far_b, before, out):
    y = pl.program_id(0)
    few = far_a.shape[0]
    features = own.shape[1]
    chunk = min(features, 64)
    place = [places[x, y] for x in range(4)]
    slot = [jnp.maximum(p, 0) // 2 for p in place]
    for start in range(0, features, chunk):
        rows = slice(start, start + chunk)
        far = jnp.where(
            slot[2] < few,
            far_a[jnp.minimum(slot[2], few - 1), rows],
            far_b[jnp.maximum(slot[2] - few, 0), rows],
        )
        values = (own[slot[0], rows], after[slot[1], rows], far, before[slot[3], rows])
        values = [value.astype(F32) for value in values]
        for b in range(2):
            total = 0.0
            for p, value in zip(place, values):
                total += jnp.where((p >= 0) & (p % 2 == b), value, 0.0)
            out[0, rows, b * BLK : (b + 1) * BLK] = total.astype(BF16)


def on_device(activations, weight, enc_bias, dec_bias, block_ids, counts):
    rows, width = activations.shape
    owners = lax.axis_size("latent")
    groups = lax.axis_size("dp")
    share = rows // groups
    chips = groups // 2
    half = rows // 2
    slots = block_ids.shape[1]
    latents = slots * BLK
    myself = lax.axis_index("latent")
    core = lax.axis_index("dp") % 2
    same_core = [[2 * z + c for z in range(chips)] for c in range(2)]
    swap = [(q, q ^ 1) for q in range(groups)]
    across = 4
    down = owners // across
    same_x = [[x * down + y for y in range(down)] for x in range(across)]
    same_y = [[x * down + y for x in range(across)] for y in range(down)]
    my_x, my_y = myself // down, myself % down
    cut = width // 2
    next_x = [(j, (j + down) % owners) for j in range(owners)]
    last_x = [(j, (j - down) % owners) for j in range(owners)]

    def across_chips(array):
        return lax.all_to_all(array, "dp", 0, 0, tiled=True, axis_index_groups=same_core)

    def shape(dims, dtype):
        return jax.ShapeDtypeStruct(dims, dtype)

    column = lax.all_gather(weight, "latent", axis=0, axis_index_groups=same_x)

    ids = block_ids[0]
    note = jnp.concatenate([ids, counts])
    note = jnp.pad(note, (0, BLK - slots - 1))
    notes = lax.all_to_all(
        jnp.broadcast_to(note, (owners, 8, BLK)), "latent", 0, 0, tiled=True
    )[:, 0, :]
    row_notes = lax.dynamic_index_in_dim(
        notes.reshape(across, down, BLK), my_y, 1, keepdims=False
    )
    row_ids = row_notes[:, :slots]
    row_live = jnp.arange(slots)[None, :] < row_notes[:, slots : slots + 1]
    column_owners = my_x * down + jnp.arange(down)
    match = row_ids[:, None, :] // 2 == column_owners[None, :, None]
    upper = jnp.any(match & (row_ids % 2 == 1)[:, None, :], axis=2)
    code = jnp.arange(slots)[None, :] * 2 + row_ids % 2 + 1
    places = jnp.sum(jnp.where(match & row_live[:, None, :], code[:, None, :], 0), axis=2) - 1
    places = jnp.roll(places, -my_x, axis=0)

    blocks = jnp.where(
        upper[:, :, None, None], column[None, :, :, BLK:], column[None, :, :, :BLK]
    )
    blocks = lax.all_to_all(
        blocks.reshape(owners, width, BLK), "latent", 0, 0, tiled=True, axis_index_groups=same_y
    )

    live = (jnp.arange(slots) < counts[0]).astype(F32)
    live_row = jnp.repeat(live, BLK)[None, :]
    bias_row = jnp.take(enc_bias.reshape(-1, BLK), ids, axis=0).reshape(1, latents)
    x_g, x_k, c_g, c_k, c_t = call(
        prepare_kernel,
        (shape((half, width), BF16),) * 4 + (shape((width, rows), BF16),),
        [SMEM_SPEC, VMEM_SPEC, VMEM_SPEC],
        (VMEM_SPEC,) * 5,
        flops=rows * width * 4,
        bytes_accessed=rows * width * 8,
    )(core[None], activations.reshape(chips, 2, share, width), dec_bias[None, :])

    matmul = 2 * half * width * latents
    x_o, c_o, bias_o = (lax.ppermute(a, "dp", swap) for a in (x_g, c_g, dec_bias[None, :]))
    tiles = call(
        functools.partial(fetch_kernel, slots),
        shape((width, latents), BF16),
        [SMEM_SPEC, ANY_SPEC],
        VMEM_SPEC,
        bytes_accessed=2 * width * latents * 2,
        scratch=[pltpu.SemaphoreType.DMA((slots,))],
    )(ids, blocks)
    tiles_o = lax.ppermute(tiles, "dp", swap)
    part = call(
        encode_kernel,
        shape((half, latents), F32),
        [VMEM_SPEC] * 2,
        VMEM_SPEC,
        flops=matmul,
        bytes_accessed=4 * half * latents * 2,
    )(c_k, tiles)
    keep = call(
        encode_rest_kernel,
        shape((half, latents), F32),
        [VMEM_SPEC] * 3,
        VMEM_SPEC,
        flops=matmul,
        bytes_accessed=4 * half * latents * 3,
    )(c_o, tiles_o, part)
    parts = across_chips(keep.reshape(chips, share, latents))
    pre, spread = call(
        activate_kernel,
        (shape((share, latents), F32), shape((chips, share, latents), BF16)),
        [VMEM_SPEC] * 3,
        (VMEM_SPEC, VMEM_SPEC),
        bytes_accessed=half * latents * 6,
    )(parts, bias_row, live_row)
    act_k = across_chips(spread).reshape(half, latents)

    scale = 2.0 / math.sqrt(rows * owners)
    packed, out_k, out_o = call(
        functools.partial(error_kernel, scale, 1.0 / (width * groups)),
        (
            shape((half, latents + BLK), F32),
            shape((half, width), BF16),
            shape((half, width), BF16),
        ),
        [VMEM_SPEC] * 7,
        (VMEM_SPEC,) * 3,
        flops=4 * matmul,
        bytes_accessed=half * latents * 14,
    )(act_k, tiles, tiles_o, x_k, x_o, dec_bias[None, :], bias_o)
    parts = across_chips(packed.astype(jnp.float16).reshape(chips, share, latents + BLK))
    act_g = lax.ppermute(act_k, "dp", swap)
    out_g = lax.ppermute(out_o, "dp", swap)
    second = call(
        second_kernel,
        shape((width, latents), F32),
        [VMEM_SPEC] * 4,
        VMEM_SPEC,
        flops=2 * matmul,
        bytes_accessed=half * latents * 16,
    )(out_g, out_k, act_g, act_k)
    spread, loss = call(
        gate_kernel,
        (shape((chips, share, latents), BF16), shape((share, BLK), F32)),
        [VMEM_SPEC] * 3,
        (VMEM_SPEC, VMEM_SPEC),
        bytes_accessed=half * latents * 6,
    )(parts.astype(F32), pre, live_row)
    row_error = loss[:, 0]
    gp_k = across_chips(spread).reshape(half, latents)
    gp_g = lax.ppermute(gp_k, "dp", swap)

    halves = call(
        functools.partial(contribution_kernel, slots),
        (shape((slots, cut, BLK), BF16), shape((slots, width - cut, BLK), BF16)),
        [VMEM_SPEC] * 4,
        (VMEM_SPEC, VMEM_SPEC),
        flops=2 * matmul,
        bytes_accessed=half * latents * 16,
    )(c_t, gp_g, gp_k, second)

    few = slots // 2
    grads = []
    for part in halves:
        before = lax.ppermute(part, "latent", next_x)
        after = lax.ppermute(part, "latent", last_x)
        far_a = lax.ppermute(after[:few], "latent", last_x)
        far_b = lax.ppermute(before[few:], "latent", next_x)
        features = part.shape[1]
        sums = pl.pallas_call(
            combine_kernel,
            grid=(down,),
            in_specs=[SMEM_SPEC] + [VMEM_SPEC] * 5,
            out_specs=pl.BlockSpec((1, features, 2 * BLK), lambda y: (y, 0, 0)),
            out_shape=shape((down, features, 2 * BLK), BF16),
            compiler_params=pltpu.CompilerParams(vmem_limit_bytes=VMEM_LIMIT),
            cost_estimate=pl.CostEstimate(
                flops=owners * features * BLK,
                bytes_accessed=owners * features * BLK * 2,
                transcendentals=0,
            ),
        )(places, part, after, far_a, far_b, before)
        sums = lax.all_to_all(sums, "latent", 0, 0, tiled=True, axis_index_groups=same_x)
        grads.append(jnp.sum(sums.astype(F32), axis=0))
    weight_grad = jnp.concatenate(grads, axis=0)
    return (weight_grad, row_error)


def solution(mesh):
    placed = (P("latent", "dp"), P("dp", "latent"), P(), P("dp"), P("latent", None), P("latent"))
    return jax.shard_map(
        on_device,
        mesh=mesh,
        in_specs=placed,
        out_specs=(P("dp", "latent"), P(("latent", "dp"))),
        check_vma=False,
    )
```

```python
import functools
import math

import jax
import jax.numpy as jnp
from jax import lax
from jax.experimental import pallas as pl
from jax.experimental.pallas import tpu as pltpu
from jax.sharding import PartitionSpec as P

BLK = 128
BF16 = jnp.bfloat16
F32 = jnp.float32
VMEM_LIMIT = 20 * 1024 * 1024
SMEM_SPEC = pl.BlockSpec(memory_space=pltpu.SMEM)
VMEM_SPEC = pl.BlockSpec(memory_space=pltpu.VMEM)
ANY_SPEC = pl.BlockSpec(memory_space=pl.ANY)


def contract(a, b, dim_a, dim_b):
    return lax.dot_general(a, b, (((dim_a,), (dim_b,)), ((), ())), preferred_element_type=F32)


def call(kernel, out_shape, in_specs, out_specs, flops=0, bytes_accessed=0, scratch=(), **more):
    return pl.pallas_call(
        kernel,
        out_shape=out_shape,
        in_specs=in_specs,
        out_specs=out_specs,
        scratch_shapes=list(scratch),
        compiler_params=pltpu.CompilerParams(vmem_limit_bytes=VMEM_LIMIT),
        cost_estimate=pl.CostEstimate(
            flops=flops, bytes_accessed=bytes_accessed, transcendentals=0
        ),
        **more,
    )


def prepare_kernel(which, x, bias, x_g, x_k, c_g, c_k, c_t):
    half = x_g.shape[0]
    core = which[0]
    for i, (part, out) in enumerate(((x_g, c_g), (x_k, c_k))):
        rows = x[:, (1 - core) if i == 0 else core].reshape(part.shape)
        part[...] = rows
        centered = rows.astype(F32) - bias[...]
        out[...] = centered.astype(BF16)
        c_t[:, i * half : (i + 1) * half] = centered.T.astype(BF16)


def fetch_kernel(slots, ids, blocks, tiles, sems):
    copies = []
    for s in range(slots):
        copy = pltpu.make_async_copy(
            blocks.at[ids[s] // 2], tiles.at[:, pl.ds(s * BLK, BLK)], sems.at[s]
        )
        copy.start()
        copies.append(copy)
    for copy in copies:
        copy.wait()


def encode_kernel(rows, tiles, out):
    for start in range(0, out.shape[1], 2 * BLK):
        columns = slice(start, start + 2 * BLK)
        out[:, columns] = contract(rows[...], tiles[:, columns], 1, 0)


def encode_rest_kernel(rows, tiles, part, out):
    for start in range(0, out.shape[1], 2 * BLK):
        columns = slice(start, start + 2 * BLK)
        out[:, columns] = contract(rows[...], tiles[:, columns], 1, 0) + part[:, columns]


def activate_kernel(parts, bias, live, pre, spread):
    total = jnp.sum(parts[...], axis=0) + bias[...]
    pre[...] = total
    act = (jnp.maximum(total, 0.0) * live[...]).astype(BF16)
    spread[...] = jnp.broadcast_to(act[None], spread.shape)


def power_above(x):
    return jnp.ceil(jnp.log2(jnp.maximum(x, 1e-30)))


def error_kernel(
    scale, loss_scale, act, tiles, tiles_o, x, x_o, bias, bias_o, out, grad_out, grad_out_o, held, sems
):
    latents = tiles.shape[1]
    loss = 0.0
    grads = []
    copies = []
    for i, rows in enumerate((x, x_o)):
        copy = pltpu.make_async_copy(rows, held.at[i], sems.at[i])
        copy.start()
        copies.append(copy)
    for i, (w, b, g) in enumerate(((tiles, bias, grad_out), (tiles_o, bias_o, grad_out_o))):
        err = contract(act[...], w[...], 1, 1) + b[...]
        copies[i].wait()
        err = err - held[i].astype(F32)
        loss += jnp.sum(err * err, axis=1, keepdims=True) * loss_scale
        grad = (err * scale).astype(BF16)
        g[...] = grad
        grads.append(grad)
    total = contract(grads[0], tiles[...], 1, 0) + contract(grads[1], tiles_o[...], 1, 0)
    top = power_above(jnp.max(jnp.abs(total), axis=1, keepdims=True))
    power = power_above(loss)
    scaled = loss * jnp.exp2(-power)
    first = scaled.astype(BF16).astype(F32)
    rest = (scaled - first) * 256.0
    lane = lax.broadcasted_iota(jnp.int32, (total.shape[0], BLK), 1)
    out[:, :latents] = total * jnp.exp2(14.0 - top)
    out[:, latents:] = jnp.where(
        lane == 0, top, jnp.where(lane == 1, power, jnp.where(lane == 2, first, rest))
    )


def second_kernel(out_g, out_k, act_g, act_k, second):
    latents = act_g.shape[1]
    for start in range(0, latents, 2 * BLK):
        columns = slice(start, start + 2 * BLK)
        second[:, columns] = contract(out_k[...], act_k[:, columns], 0, 0) + contract(
            out_g[...], act_g[:, columns], 0, 0
        )


def gate_kernel(parts, pre, live, second, spread, loss):
    chips, _, width = parts.shape
    latents = width - BLK
    total = jnp.zeros(pre.shape, F32)
    error = jnp.zeros(loss.shape, F32)
    for z in range(chips):
        extra = parts[z, :, latents:]
        total += parts[z, :, :latents] * jnp.exp2(extra[:, :1] - 14.0)
        row = (extra[:, 2:3] + extra[:, 3:4] * (1.0 / 256.0)) * jnp.exp2(extra[:, 1:2])
        error += jnp.broadcast_to(row, loss.shape)
    grad = (jnp.where(pre[...] > 0, total, 0.0) * live[...]).astype(BF16)
    spread[...] = jnp.broadcast_to(grad[None], spread.shape)
    loss[...] = error


def contribution_kernel(slots, c_t, gp_g, gp_k, second, low, high):
    half = gp_g.shape[0]
    cut = low.shape[1]
    for s in range(0, slots, 2):
        columns = slice(s * BLK, (s + 2) * BLK)
        total = (
            contract(c_t[:, :half], gp_g[:, columns], 1, 0)
            + contract(c_t[:, half:], gp_k[:, columns], 1, 0)
            + second[:, columns]
        ).astype(BF16)
        for i in range(s, s + 2):
            part = total[:, (i - s) * BLK : (i - s + 1) * BLK]
            low[i] = part[:cut]
            high[i] = part[cut:]


def combine_kernel(places, own, after, far_a, far_b, before, out):
    few = far_a.shape[0]
    features = own.shape[1]
    chunk = min(features, 64)

    def one_owner(y, carry):
        place = [places[x, y] for x in range(4)]
        slot = [jnp.maximum(p, 0) // 2 for p in place]
        for start in range(0, features, chunk):
            rows = slice(start, start + chunk)
            far = jnp.where(
                slot[2] < few,
                far_a[jnp.minimum(slot[2], few - 1), rows],
                far_b[jnp.maximum(slot[2] - few, 0), rows],
            )
            values = (own[slot[0], rows], after[slot[1], rows], far, before[slot[3], rows])
            values = [value.astype(F32) for value in values]
            for b in range(2):
                total = 0.0
                for p, value in zip(place, values):
                    total += jnp.where((p >= 0) & (p % 2 == b), value, 0.0)
                out[y, rows, b * BLK : (b + 1) * BLK] = total.astype(BF16)
        return carry

    lax.fori_loop(0, out.shape[0], one_owner, 0)


def on_device(activations, weight, enc_bias, dec_bias, block_ids, counts):
    rows, width = activations.shape
    owners = lax.axis_size("latent")
    groups = lax.axis_size("dp")
    share = rows // groups
    chips = groups // 2
    half = rows // 2
    slots = block_ids.shape[1]
    latents = slots * BLK
    myself = lax.axis_index("latent")
    core = lax.axis_index("dp") % 2
    same_core = [[2 * z + c for z in range(chips)] for c in range(2)]
    swap = [(q, q ^ 1) for q in range(groups)]
    across = 4
    down = owners // across
    same_x = [[x * down + y for y in range(down)] for x in range(across)]
    same_y = [[x * down + y for x in range(across)] for y in range(down)]
    my_x, my_y = myself // down, myself % down
    cut = width // 2
    next_x = [(j, (j + down) % owners) for j in range(owners)]
    last_x = [(j, (j - down) % owners) for j in range(owners)]

    def across_chips(array):
        return lax.all_to_all(array, "dp", 0, 0, tiled=True, axis_index_groups=same_core)

    def shape(dims, dtype):
        return jax.ShapeDtypeStruct(dims, dtype)

    column = lax.all_gather(weight, "latent", axis=0, axis_index_groups=same_x)

    ids = block_ids[0]
    note = jnp.concatenate([ids, counts])
    note = jnp.pad(note, (0, BLK - slots - 1))
    notes = lax.all_to_all(
        jnp.broadcast_to(note, (owners, 8, BLK)), "latent", 0, 0, tiled=True
    )[:, 0, :]
    row_notes = lax.dynamic_index_in_dim(
        notes.reshape(across, down, BLK), my_y, 1, keepdims=False
    )
    row_ids = row_notes[:, :slots]
    row_live = jnp.arange(slots)[None, :] < row_notes[:, slots : slots + 1]
    column_owners = my_x * down + jnp.arange(down)
    match = row_ids[:, None, :] // 2 == column_owners[None, :, None]
    upper = jnp.any(match & (row_ids % 2 == 1)[:, None, :], axis=2)
    code = jnp.arange(slots)[None, :] * 2 + row_ids % 2 + 1
    places = jnp.sum(jnp.where(match & row_live[:, None, :], code[:, None, :], 0), axis=2) - 1
    places = jnp.roll(places, -my_x, axis=0)

    x_g, x_k, c_g, c_k, c_t = call(
        prepare_kernel,
        (shape((half, width), BF16),) * 4 + (shape((width, rows), BF16),),
        [SMEM_SPEC, VMEM_SPEC, VMEM_SPEC],
        (VMEM_SPEC,) * 5,
        flops=rows * width * 4,
        bytes_accessed=rows * width * 8,
    )(core[None], activations.reshape(chips, 2, share, width), dec_bias[None, :])
    x_o, c_o, bias_o = (lax.ppermute(a, "dp", swap) for a in (x_g, c_g, dec_bias[None, :]))
    upper, x_o, c_o, bias_o = lax.optimization_barrier((upper, x_o, c_o, bias_o))

    blocks = jnp.where(
        upper[:, :, None, None], column[None, :, :, BLK:], column[None, :, :, :BLK]
    )
    blocks = lax.all_to_all(
        blocks.reshape(owners, width, BLK), "latent", 0, 0, tiled=True, axis_index_groups=same_y
    )

    live = (jnp.arange(slots) < counts[0]).astype(F32)
    live_row = jnp.repeat(live, BLK)[None, :]
    bias_row = jnp.take(enc_bias.reshape(-1, BLK), ids, axis=0).reshape(1, latents)
    matmul = 2 * half * width * latents
    tiles = call(
        functools.partial(fetch_kernel, slots),
        shape((width, latents), BF16),
        [SMEM_SPEC, ANY_SPEC],
        VMEM_SPEC,
        bytes_accessed=2 * width * latents * 2,
        scratch=[pltpu.SemaphoreType.DMA((slots,))],
    )(ids, blocks)
    tiles_o = lax.ppermute(tiles, "dp", swap)
    part = call(
        encode_kernel,
        shape((half, latents), F32),
        [VMEM_SPEC] * 2,
        VMEM_SPEC,
        flops=matmul,
        bytes_accessed=4 * half * latents * 2,
    )(c_k, tiles)
    keep = call(
        encode_rest_kernel,
        shape((half, latents), F32),
        [VMEM_SPEC] * 3,
        VMEM_SPEC,
        flops=matmul,
        bytes_accessed=4 * half * latents * 3,
    )(c_o, tiles_o, part)
    parts = across_chips(keep.reshape(chips, share, latents))
    pre, spread = call(
        activate_kernel,
        (shape((share, latents), F32), shape((chips, share, latents), BF16)),
        [VMEM_SPEC] * 3,
        (VMEM_SPEC, VMEM_SPEC),
        bytes_accessed=half * latents * 6,
    )(parts, bias_row, live_row)
    act_k = across_chips(spread).reshape(half, latents)

    scale = 2.0 / math.sqrt(rows * owners)
    packed, out_k, out_o = call(
        functools.partial(error_kernel, scale, 1.0 / (width * groups)),
        (
            shape((half, latents + BLK), F32),
            shape((half, width), BF16),
            shape((half, width), BF16),
        ),
        [VMEM_SPEC] * 3 + [ANY_SPEC] * 2 + [VMEM_SPEC] * 2,
        (VMEM_SPEC,) * 3,
        flops=4 * matmul,
        bytes_accessed=half * latents * 14,
        scratch=[pltpu.VMEM((2, half, width), BF16), pltpu.SemaphoreType.DMA((2,))],
    )(act_k, tiles, tiles_o, x_k, x_o, dec_bias[None, :], bias_o)
    parts = across_chips(packed.astype(jnp.float16).reshape(chips, share, latents + BLK))
    act_g = lax.ppermute(act_k, "dp", swap)
    out_g = lax.ppermute(out_o, "dp", swap)
    second = call(
        second_kernel,
        shape((width, latents), F32),
        [VMEM_SPEC] * 4,
        VMEM_SPEC,
        flops=2 * matmul,
        bytes_accessed=half * latents * 16,
    )(out_g, out_k, act_g, act_k)
    spread, loss = call(
        gate_kernel,
        (shape((chips, share, latents), BF16), shape((share, BLK), F32)),
        [VMEM_SPEC] * 3 + [ANY_SPEC],
        (VMEM_SPEC, VMEM_SPEC),
        bytes_accessed=half * latents * 6,
    )(parts.astype(F32), pre, live_row, second)
    row_error = loss[:, 0]
    gp_k = across_chips(spread).reshape(half, latents)
    gp_g = lax.ppermute(gp_k, "dp", swap)

    halves = call(
        functools.partial(contribution_kernel, slots),
        (shape((slots, cut, BLK), BF16), shape((slots, width - cut, BLK), BF16)),
        [VMEM_SPEC] * 4,
        (VMEM_SPEC, VMEM_SPEC),
        flops=2 * matmul,
        bytes_accessed=half * latents * 16,
    )(c_t, gp_g, gp_k, second)

    few = slots // 2
    grads = []
    for part in halves:
        before = lax.ppermute(part, "latent", next_x)
        after = lax.ppermute(part, "latent", last_x)
        far_a = lax.ppermute(after[:few], "latent", last_x)
        far_b = lax.ppermute(before[few:], "latent", next_x)
        features = part.shape[1]
        sums = call(
            combine_kernel,
            shape((down, features, 2 * BLK), BF16),
            [SMEM_SPEC] + [VMEM_SPEC] * 5,
            VMEM_SPEC,
            flops=owners * features * BLK,
            bytes_accessed=owners * features * BLK * 2,
        )(places, part, after, far_a, far_b, before)
        sums = lax.all_to_all(sums, "latent", 0, 0, tiled=True, axis_index_groups=same_x)
        grads.append(jnp.sum(sums.astype(F32), axis=0))
    weight_grad = jnp.concatenate(grads, axis=0)
    return (weight_grad, row_error)


def solution(mesh):
    placed = (P("latent", "dp"), P("dp", "latent"), P(), P("dp"), P("latent", None), P("latent"))
    return jax.shard_map(
        on_device,
        mesh=mesh,
        in_specs=placed,
        out_specs=(P("dp", "latent"), P(("latent", "dp"))),
        check_vma=False,
    )
```
